256 devices in a mesh: dp: 64 (over z, y, core), mp: 4 (over x).
Axes of the slice: x: 4, y: 4, z: 8, core: 2. Of those that a mesh axis runs over, the one named last changes fastest.
Arguments:
- features: bfloat16 [32768, 8192], P('dp', 'mp'), may hold values from -6 to 6
- grad_out: bfloat16 [32768, 28672], P('dp', 'mp'), may hold values from -0.005859375 to 0.005859375
- basis: bfloat16 [8192, 256], P('dp'), may hold values from -0.375 to 0.375
- first_moment: float32 [256, 28672], P('dp', 'mp'), may hold values from -6 to 6
- second_moment: float32 [256, 28672], P('dp', 'mp'), may hold values from 0.1 to 10
Outputs:
- delta: bfloat16 [8192, 28672], P('dp', 'mp')
- new_first: float32 [256, 28672], P('dp', 'mp')
- new_second: float32 [256, 28672], P('dp', 'mp')
The draws below stay inside these ranges and needn't reach their ends.
All inputs are finite; a program needn't handle non-finite values.
Results may differ from the reference program's by a relative error of at most 0.005.
Values may be sent and summed in bfloat16 or wider, within the bound.
No kernel may reach another device: no remote copies, remote signals or barrier semaphores. Data moves between devices by JAX's collectives and lax.ppermute only.
A program may use at most 128 MiB of HBM per device.

```python
import math
import jax
import jax.numpy as jnp

D = 8192
FF = 28672
R = 256
STEP = 100
TOKENS = 32768


def shard_levels(stream_key, extent, shards, least, high):
    factor_of, own = 1.0, jax.random.fold_in(stream_key, 6)
    for axis_at, blocks in shards:
        steps = jnp.exp(jax.random.uniform(jax.random.fold_in(own, axis_at), (blocks,), jnp.float32, least / len(shards), high / len(shards)))
        factor_of = factor_of * jnp.repeat(steps, extent[axis_at] // blocks).reshape([-1 if axis == axis_at else 1 for axis in range(len(extent))])
    return factor_of


def noise(stream_key, extent, spread, reach, split=(), held_as=jnp.bfloat16):
    result = spread * jax.random.normal(stream_key, extent, jnp.float32)
    if split:
        result = result * shard_levels(stream_key, extent, split, -0.22, 0.18)
    return jnp.clip(result, -reach, reach).astype(held_as)


def setup_inputs(seed: int = 0) -> dict:
    streams_of = jax.random.split(jax.random.key(seed), 6)
    features = noise(streams_of[0], (TOKENS, D), 1.0, 6.0, ((0, 64), (1, 4)))
    grad_out = noise(streams_of[1], (TOKENS, FF), ((R / (D * TOKENS)) ** 0.5), 0.005859375, ((0, 64), (1, 4)))
    basis = noise(streams_of[2], (D, R), R ** -0.5, 0.375, ((0, 64),))
    first_moment = noise(streams_of[3], (R, FF), 1.0, 6.0, ((0, 64), (1, 4)), jnp.float32)
    second_moment = jnp.clip(jnp.exp(math.log(10.0) - 4.6051702 * jax.random.uniform(streams_of[4], (R, FF), jnp.float32) ** shard_levels(streams_of[4], (R, FF), ((0, 64), (1, 4)), -0.2, 0.2)), 0.1, 10.0)
    return dict(features=features, grad_out=grad_out, basis=basis, first_moment=first_moment, second_moment=second_moment)


first_decay = 0.9
second_decay = 0.999
epsilon_term = 1e-08

def reference(features, grad_out, basis, first_moment, second_moment):
    projected = jnp.dot(features, basis, preferred_element_type=jnp.float32).astype(jnp.bfloat16)
    lowrank = jnp.dot(projected.T, grad_out, preferred_element_type=jnp.float32)
    new_first = first_decay * first_moment + (1.0 - first_decay) * lowrank
    new_second = second_decay * second_moment + (1.0 - second_decay) * lowrank * lowrank
    first_fix = 1.0 - first_decay ** STEP
    second_fix = 1.0 - second_decay ** STEP
    normalized = (new_first / first_fix / (jnp.sqrt(new_second / second_fix) + epsilon_term)).astype(jnp.bfloat16)
    delta = jnp.dot(basis, normalized, preferred_element_type=jnp.float32).astype(jnp.bfloat16)
    return (delta, new_first, new_second)
```

```python
import functools

import jax
import jax.numpy as jnp
import numpy as np
from jax import lax
from jax.experimental import pallas as pl
from jax.experimental.pallas import tpu as pltpu
from jax.sharding import Mesh, PartitionSpec as P

STEP = 100

first_decay = 0.9
second_decay = 0.999
epsilon_term = 1e-08

Z, Y, C, X = 8, 4, 2, 4
ALL = ("z", "y", "c", "x")
DP = ("z", "y", "c")


def place(z, y, c):
    return (z * Y + y) * C + c


def paired(i, size, offset, far):
    return (i + far) % size if (i + offset) % 2 == 0 else (i - far) % size


def partner(step, z, y, c):
    axis, offset, far = step
    if axis == "c":
        return z, y, 1 - c
    if axis == "z":
        return paired(z, Z, offset + c, far), y, c
    return z, paired(y, Y, offset + c, far), c


CHAINS = (
    (("c", 0, 0), ("y", 0, 1), ("y", 1, 1), ("z", 0, 1), ("z", 1, 1), ("z", 0, 3)),
    (("c", 0, 0), ("z", 0, 1), ("z", 1, 1), ("z", 0, 3), ("y", 0, 1), ("y", 1, 1)),
)
COORDS = [(z, y, c) for z in range(Z) for y in range(Y) for c in range(C)]


def swap(step):
    return [(place(*at), place(*partner(step, *at))) for at in COORDS]


def orders(steps):
    held = {at: [place(*at)] for at in COORDS}
    for step in reversed(steps):
        held = {at: held[at] + held[partner(step, *at)] for at in COORDS}
    for blocks in held.values():
        assert sorted(blocks) == list(range(Z * Y * C))
    return np.array([held[at] for at in COORDS], np.int32)


def rank_table(rows):
    blocks = np.stack([orders(steps) for steps in CHAINS], 1)
    return (blocks[..., None] * rows + np.arange(rows, dtype=np.int32)).reshape(Z * Y * C, len(CHAINS), -1)


def crossing(flip):
    full = lambda z, y, c, x: place(z, y, c) * X + x
    return [
        (full(2 * x + (b ^ flip), y, c, q), full(2 * q + b, y, c, x))
        for x in range(X) for q in range(Z // 2) for b in range(2) for y in range(Y) for c in range(C)
    ]


def lowrank_body(left_ref, grad_ref, keep_ref, send_ref):
    product = jnp.dot(left_ref[0], grad_ref[...], preferred_element_type=jnp.float32)
    half = keep_ref.shape[0]
    keep_ref[...] = product[:half]
    send_ref[...] = product[half:].astype(send_ref.dtype)


def lowrank_part(left, grad_out, half):
    ranks, tokens = left.shape[1:]
    columns = grad_out.shape[1] // len(CHAINS)
    tiles = 4
    wide = columns // tiles
    return pl.pallas_call(
        lowrank_body,
        grid=(tiles,),
        in_specs=[
            pl.BlockSpec((1, ranks, tokens), lambda j: (half, 0, 0)),
            pl.BlockSpec((tokens, wide), lambda j: (0, half * tiles + j)),
        ],
        out_specs=[pl.BlockSpec((ranks // 2, wide), lambda j: (0, j))] * 2,
        out_shape=[
            jax.ShapeDtypeStruct((ranks // 2, columns), jnp.float32),
            jax.ShapeDtypeStruct((ranks // 2, columns), jnp.bfloat16),
        ],
        cost_estimate=pl.CostEstimate(
            flops=2 * ranks * tokens * columns, bytes_accessed=tokens * columns * 2 + ranks * columns * 3, transcendentals=0
        ),
        name="lowrank_part",
    )(left, grad_out)


def delta_body(tiles, basis_ref, own_a, other_a, own_b, other_b, out_ref):
    def put(half, own, other):
        ranks = own.shape[0]
        total = jnp.dot(basis_ref[half, :, :ranks], own[...], preferred_element_type=jnp.float32)
        total += jnp.dot(basis_ref[half, :, ranks:], other[...], preferred_element_type=jnp.float32)
        out_ref[...] = total.astype(out_ref.dtype)

    @pl.when(pl.program_id(0) < tiles)
    def _():
        put(0, own_a, other_a)

    @pl.when(pl.program_id(0) >= tiles)
    def _():
        put(1, own_b, other_b)


def delta_product(basis, own_a, other_a, own_b, other_b):
    ranks, columns = own_a.shape
    rows = basis.shape[1]
    tiles = 4
    wide = columns // tiles
    first = pl.BlockSpec((ranks, wide), lambda j: (0, jnp.minimum(j, tiles - 1)))
    second = pl.BlockSpec((ranks, wide), lambda j: (0, jnp.maximum(j - tiles, 0)))
    return pl.pallas_call(
        functools.partial(delta_body, tiles),
        grid=(2 * tiles,),
        in_specs=[pl.BlockSpec(basis.shape, lambda j: (0, 0, 0)), first, first, second, second],
        out_specs=pl.BlockSpec((rows, wide), lambda j: (0, j)),
        out_shape=jax.ShapeDtypeStruct((rows, 2 * columns), jnp.bfloat16),
        cost_estimate=pl.CostEstimate(
            flops=8 * ranks * rows * columns, bytes_accessed=(8 * ranks + 4 * rows) * columns, transcendentals=0
        ),
        name="delta_product",
    )(basis, own_a, other_a, own_b, other_b)


def gathered_basis(basis):
    z, y, c = (lax.axis_index(a) for a in DP)
    odd = z % 2 == 1
    same, flipped = (lax.ppermute(basis, ALL, crossing(flip)) for flip in (0, 1))
    pair = jnp.stack([jnp.where(odd, flipped, same), jnp.where(odd, same, flipped)])
    whole = jnp.zeros((Y, *pair.shape), basis.dtype)
    whole = lax.dynamic_update_slice_in_dim(whole, pair[None], y, 0)
    for far in (1, 3, 2):
        came = lax.ppermute(pair, "y", [(i, (i + far) % Y) for i in range(Y)])
        whole = lax.dynamic_update_slice_in_dim(whole, came[None], (y + Y - far) % Y, 0)
    other = lax.ppermute(whole, "c", [(0, 1), (1, 0)])
    first = c == 0
    both = jnp.stack([jnp.where(first, whole, other), jnp.where(first, other, whole)])
    return both.transpose(2, 1, 0, 3, 4).reshape(-1, basis.shape[1])


def x_pairs(offset):
    return [(c * X + x, c * X + paired(x, X, offset + c, 1)) for c in range(C) for x in range(X)]


def on_device(features, grad_out, basis, first_moment, second_moment):
    me = place(*(lax.axis_index(a) for a in DP))
    rows = first_moment.shape[0]
    table = lax.dynamic_index_in_dim(jnp.asarray(rank_table(rows)), me, 0, keepdims=False)
    ranks = table.shape[1]
    chosen = (lax.broadcasted_iota(jnp.int32, (len(CHAINS), ranks, ranks), 1) == table[:, None, :]).astype(jnp.bfloat16)
    ordered_basis = jnp.einsum("dr,krp->kdp", basis, chosen, preferred_element_type=jnp.float32).astype(jnp.bfloat16)

    total = jnp.dot(features, gathered_basis(basis), preferred_element_type=jnp.float32)
    for offset in (0, 1):
        total = total + lax.ppermute(total.astype(jnp.bfloat16), ("c", "x"), x_pairs(offset)).astype(jnp.float32)
    projected = total.astype(jnp.bfloat16)
    left = jnp.einsum("krp,tr->kpt", chosen, projected, preferred_element_type=jnp.float32).astype(jnp.bfloat16)

    parts = [lowrank_part(left, grad_out, half) for half in range(len(CHAINS))]
    keep, send = [list(t) for t in zip(*parts)]
    for at in range(len(CHAINS[0])):
        for k, steps in enumerate(CHAINS):
            came = lax.ppermute(send[k], DP, swap(steps[at]))
            half = came.shape[0] // 2
            if at + 1 < len(steps):
                send[k] = (keep[k][half:] + came[half:].astype(jnp.float32)).astype(jnp.bfloat16)
                keep[k] = keep[k][:half] + came[:half].astype(jnp.float32)
            else:
                keep[k] = keep[k] + came.astype(jnp.float32)

    first_fix = 1.0 - first_decay**STEP
    second_fix = 1.0 - second_decay**STEP
    columns = keep[0].shape[1]
    firsts, seconds, held = [], [], []
    for k, lowrank in enumerate(keep):
        span = slice(k * columns, (k + 1) * columns)
        new_first = first_decay * first_moment[:, span] + (1.0 - first_decay) * lowrank
        new_second = second_decay * second_moment[:, span] + (1.0 - second_decay) * lowrank * lowrank
        normalized = (
            new_first / first_fix / (jnp.sqrt(new_second / second_fix) + epsilon_term)
        ).astype(jnp.bfloat16)
        firsts.append(new_first)
        seconds.append(new_second)
        held.append(normalized)

    for at in reversed(range(1, len(CHAINS[0]))):
        for k, steps in enumerate(CHAINS):
            came = lax.ppermute(held[k], DP, swap(steps[at]))
            held[k] = jnp.concatenate([held[k], came], 0)
    others = [lax.ppermute(held[k], DP, swap(steps[0])) for k, steps in enumerate(CHAINS)]
    delta = delta_product(ordered_basis, held[0], others[0], held[1], others[1])
    return (delta, jnp.concatenate(firsts, 1), jnp.concatenate(seconds, 1))


def solution(mesh):
    fine = Mesh(mesh.devices.reshape(Z, Y, C, X), ALL)
    rows_columns = P(DP, "x")
    in_specs = (rows_columns, rows_columns, P(DP, None), rows_columns, rows_columns)
    return jax.shard_map(
        on_device, mesh=fine, in_specs=in_specs, out_specs=(rows_columns,) * 3, check_vma=False
    )
```

```python
import functools

import jax
import jax.numpy as jnp
import numpy as np
from jax import lax
from jax.experimental import pallas as pl
from jax.experimental.pallas import tpu as pltpu
from jax.sharding import Mesh, PartitionSpec as P

STEP = 100

first_decay = 0.9
second_decay = 0.999
epsilon_term = 1e-08

Z, Y, C, X = 8, 4, 2, 4
KERNEL_VMEM = 16 * 1024 * 1024
ALL = ("z", "y", "c", "x")
DP = ("z", "y", "c")


def place(z, y, c):
    return (z * Y + y) * C + c


def paired(i, size, offset, far):
    return (i + far) % size if (i + offset) % 2 == 0 else (i - far) % size


def partner(step, z, y, c):
    axis, offset, far = step
    if axis == "c":
        return z, y, 1 - c
    if axis == "z":
        return paired(z, Z, offset + c, far), y, c
    return z, paired(y, Y, offset + c, far), c


CHAINS = (
    (("c", 0, 0), ("y", 0, 1), ("y", 1, 1), ("z", 0, 1), ("z", 1, 1), ("z", 0, 3)),
    (("c", 0, 0), ("z", 0, 1), ("z", 1, 1), ("y", 0, 1), ("y", 1, 1), ("z", 0, 3)),
)
COORDS = [(z, y, c) for z in range(Z) for y in range(Y) for c in range(C)]


def swap(step):
    return [(place(*at), place(*partner(step, *at))) for at in COORDS]


def orders(steps):
    held = {at: [place(*at)] for at in COORDS}
    for step in reversed(steps):
        held = {at: held[at] + held[partner(step, *at)] for at in COORDS}
    for blocks in held.values():
        assert sorted(blocks) == list(range(Z * Y * C))
    return np.array([held[at] for at in COORDS], np.int32)


def rank_table(rows):
    blocks = np.stack([orders(steps) for steps in CHAINS], 1)
    return (blocks[..., None] * rows + np.arange(rows, dtype=np.int32)).reshape(Z * Y * C, len(CHAINS), -1)


def crossing(flip):
    full = lambda z, y, c, x: place(z, y, c) * X + x
    return [
        (full(2 * x + (b ^ flip), y, c, (2 * x + 2 - q) % X), full(2 * q + b, y, c, x))
        for x in range(X) for q in range(Z // 2) for b in range(2) for y in range(Y) for c in range(C)
    ]


def lowrank_body(left_ref, grad_ref, out_ref):
    out_ref[...] = jnp.dot(left_ref[...], grad_ref[...], preferred_element_type=jnp.float32).astype(out_ref.dtype)


def lowrank_part(left, grad_out, at, parts, kind):
    ranks, tokens = left.shape
    columns = grad_out.shape[1] // parts
    tiles = 4 // parts
    wide = columns // tiles
    return pl.pallas_call(
        lowrank_body,
        grid=(tiles,),
        in_specs=[
            pl.BlockSpec((ranks, tokens), lambda j: (0, 0)),
            pl.BlockSpec((tokens, wide), lambda j: (0, at * tiles + j)),
        ],
        out_specs=pl.BlockSpec((ranks, wide), lambda j: (0, j)),
        out_shape=jax.ShapeDtypeStruct((ranks, columns), kind),
        compiler_params=pltpu.CompilerParams(vmem_limit_bytes=KERNEL_VMEM),
        cost_estimate=pl.CostEstimate(
            flops=2 * ranks * tokens * columns, bytes_accessed=tokens * columns * 2 + ranks * columns * 4, transcendentals=0
        ),
        name="lowrank_part",
    )(left, grad_out)


def delta_body(tiles, basis_ref, *refs):
    *held, out_ref = refs
    for k in range(len(held) // 2):
        own, other = held[2 * k : 2 * k + 2]
        ranks = own.shape[0]

        @pl.when(pl.program_id(0) // tiles == k)
        def _():
            total = jnp.dot(basis_ref[k, :, :ranks], own[...], preferred_element_type=jnp.float32)
            total += jnp.dot(basis_ref[k, :, ranks:], other[...], preferred_element_type=jnp.float32)
            out_ref[...] = total.astype(out_ref.dtype)


def delta_product(basis, held):
    parts, rows = basis.shape[:2]
    ranks, columns = held[0].shape
    tiles = 4 // parts
    wide = columns // tiles
    block = lambda k: pl.BlockSpec((ranks, wide), lambda j: (0, jnp.clip(j - k * tiles, 0, tiles - 1)))
    return pl.pallas_call(
        functools.partial(delta_body, tiles),
        grid=(parts * tiles,),
        in_specs=[pl.BlockSpec(basis.shape, lambda j: (0, 0, 0)), *(block(k // 2) for k in range(2 * parts))],
        out_specs=pl.BlockSpec((rows, wide), lambda j: (0, j)),
        out_shape=jax.ShapeDtypeStruct((rows, parts * columns), jnp.bfloat16),
        compiler_params=pltpu.CompilerParams(vmem_limit_bytes=KERNEL_VMEM),
        cost_estimate=pl.CostEstimate(
            flops=4 * parts * ranks * rows * columns, bytes_accessed=(4 * ranks + 2 * rows) * parts * columns, transcendentals=0
        ),
        name="delta_product",
    )(basis, *held)


def gathered_basis(basis):
    z, y, c = (lax.axis_index(a) for a in DP)
    odd = z % 2 == 1
    same, flipped = (lax.ppermute(basis, ALL, crossing(flip)) for flip in (0, 1))
    pair = jnp.stack([jnp.where(odd, flipped, same), jnp.where(odd, same, flipped)])
    whole = jnp.zeros((Y, *pair.shape), basis.dtype)
    whole = lax.dynamic_update_slice_in_dim(whole, pair[None], y, 0)
    for far in (1, 3, 2):
        came = lax.ppermute(pair, "y", [(i, (i + far) % Y) for i in range(Y)])
        whole = lax.dynamic_update_slice_in_dim(whole, came[None], (y + Y - far) % Y, 0)
    other = lax.ppermute(whole, "c", [(0, 1), (1, 0)])
    first = c == 0
    both = jnp.stack([jnp.where(first, whole, other), jnp.where(first, other, whole)])
    return both.transpose(2, 1, 0, 3, 4).reshape(-1, basis.shape[1])


def x_pairs(offset):
    return [(c * X + x, c * X + paired(x, X, offset + c, 1)) for c in range(C) for x in range(X)]


def on_device(features, grad_out, basis, first_moment, second_moment):
    me = place(*(lax.axis_index(a) for a in DP))
    rows = first_moment.shape[0]
    table = lax.dynamic_index_in_dim(jnp.asarray(rank_table(rows)), me, 0, keepdims=False)
    ranks = table.shape[1]
    chosen = (lax.broadcasted_iota(jnp.int32, (len(CHAINS), ranks, ranks), 1) == table[:, None, :]).astype(jnp.bfloat16)
    ordered_basis = jnp.einsum("dr,krp->kdp", basis, chosen, preferred_element_type=jnp.float32).astype(jnp.bfloat16)

    total = jnp.dot(features, gathered_basis(basis), preferred_element_type=jnp.float32)
    for offset in (0, 1):
        total = total + lax.ppermute(total.astype(jnp.bfloat16), ("c", "x"), x_pairs(offset)).astype(jnp.float32)
    projected = total.astype(jnp.bfloat16)
    left = jnp.einsum("krp,tr->kpt", chosen, projected, preferred_element_type=jnp.float32).astype(jnp.bfloat16)

    parts = len(CHAINS)
    half = ranks // 2
    send = [lowrank_part(left[k, half:], grad_out, k, parts, jnp.bfloat16) for k in range(parts)]
    keep = [lowrank_part(left[k, :half], grad_out, k, parts, jnp.float32) for k in range(parts)]
    for at in range(len(CHAINS[0])):
        for k, steps in enumerate(CHAINS):
            came = lax.ppermute(send[k], DP, swap(steps[at]))
            half = came.shape[0] // 2
            if at + 1 < len(steps):
                send[k] = (keep[k][half:] + came[half:].astype(jnp.float32)).astype(jnp.bfloat16)
                keep[k] = keep[k][:half] + came[:half].astype(jnp.float32)
            else:
                keep[k] = keep[k] + came.astype(jnp.float32)

    first_fix = 1.0 - first_decay**STEP
    second_fix = 1.0 - second_decay**STEP
    columns = keep[0].shape[1]
    firsts, seconds, held = [], [], []
    for k, lowrank in enumerate(keep):
        span = slice(k * columns, (k + 1) * columns)
        new_first = first_decay * first_moment[:, span] + (1.0 - first_decay) * lowrank
        new_second = second_decay * second_moment[:, span] + (1.0 - second_decay) * lowrank * lowrank
        normalized = (
            new_first / first_fix / (jnp.sqrt(new_second / second_fix) + epsilon_term)
        ).astype(jnp.bfloat16)
        firsts.append(new_first)
        seconds.append(new_second)
        held.append(normalized)

    for at in reversed(range(1, len(CHAINS[0]))):
        for k, steps in enumerate(CHAINS):
            came = lax.ppermute(held[k], DP, swap(steps[at]))
            held[k] = lax.optimization_barrier(jnp.concatenate([held[k], came], 0))
    last = []
    for k, steps in enumerate(CHAINS):
        last += [held[k], lax.ppermute(held[k], DP, swap(steps[0]))]
    delta = delta_product(ordered_basis, last)
    return (delta, jnp.concatenate(firsts, 1), jnp.concatenate(seconds, 1))


def solution(mesh):
    fine = Mesh(mesh.devices.reshape(Z, Y, C, X), ALL)
    rows_columns = P(DP, "x")
    in_specs = (rows_columns, rows_columns, P(DP, None), rows_columns, rows_columns)
    return jax.shard_map(
        on_device, mesh=fine, in_specs=in_specs, out_specs=(rows_columns,) * 3, check_vma=False
    )
```

```python
import functools

import jax
import jax.numpy as jnp
import numpy as np
from jax import lax
from jax.experimental import pallas as pl
from jax.experimental.pallas import tpu as pltpu
from jax.sharding import Mesh, PartitionSpec as P

STEP = 100

first_decay = 0.9
second_decay = 0.999
epsilon_term = 1e-08

Z, Y, C, X = 8, 4, 2, 4
KERNEL_VMEM = 16 * 1024 * 1024
ALL = ("z", "y", "c", "x")
DP = ("z", "y", "c")


def place(z, y, c):
    return (z * Y + y) * C + c


def paired(i, size, offset, far):
    return (i + far) % size if (i + offset) % 2 == 0 else (i - far) % size


def partner(step, z, y, c):
    axis, offset, far = step
    if axis == "c":
        return z, y, 1 - c
    if axis == "z":
        return paired(z, Z, offset + c, far), y, c
    return z, paired(y, Y, offset + c, far), c


APART = (
    (("c", 0, 0), ("y", 0, 1), ("y", 1, 1), ("z", 0, 1), ("z", 1, 1)),
    (("c", 0, 0), ("z", 0, 1), ("z", 1, 1), ("y", 0, 1), ("y", 1, 1)),
)
TOGETHER = (("z", 0, 3),)
COORDS = [(z, y, c) for z in range(Z) for y in range(Y) for c in range(C)]


def swap(step):
    return [(place(*at), place(*partner(step, *at))) for at in COORDS]


def orders(steps):
    held = {at: [place(*at)] for at in COORDS}
    for step in reversed(steps):
        held = {at: held[at] + held[partner(step, *at)] for at in COORDS}
    for blocks in held.values():
        assert sorted(blocks) == list(range(Z * Y * C))
    return np.array([held[at] for at in COORDS], np.int32)


def rank_table(rows):
    blocks = np.stack([orders(steps + TOGETHER) for steps in APART], 1)
    return (blocks[..., None] * rows + np.arange(rows, dtype=np.int32)).reshape(Z * Y * C, len(APART), -1)


def crossing(flip):
    full = lambda z, y, c, x: place(z, y, c) * X + x
    return [
        (full(2 * x + (b ^ flip), y, c, (2 * x + 2 - q) % X), full(2 * q + b, y, c, x))
        for x in range(X) for q in range(Z // 2) for b in range(2) for y in range(Y) for c in range(C)
    ]


def in_vmem(x):
    return pltpu.with_memory_space_constraint(x, pltpu.VMEM)


def lowrank_body(first, wide, left_ref, grad_ref, keep_ref, send_ref):
    half, columns = keep_ref.shape

    @pl.loop(0, columns // wide)
    def _(j):
        source = pl.ds(pl.multiple_of(first + j * wide, 128), wide)
        product = jnp.dot(left_ref[...], grad_ref[:, source], preferred_element_type=jnp.float32)
        target = pl.ds(pl.multiple_of(j * wide, 128), wide)
        keep_ref[:, target] = product[:half]
        send_ref[:, target] = product[half:].astype(send_ref.dtype)


def lowrank_part(left, grad_out, at, parts):
    ranks, tokens = left.shape
    columns = grad_out.shape[1] // parts
    whole = pl.BlockSpec(memory_space=pltpu.VMEM)
    return pl.pallas_call(
        functools.partial(lowrank_body, at * columns, columns // 4),
        in_specs=[whole] * 2,
        out_specs=[whole] * 2,
        out_shape=[pltpu.VMEM((ranks // 2, columns), jnp.float32), pltpu.VMEM((ranks // 2, columns), jnp.bfloat16)],
        compiler_params=pltpu.CompilerParams(vmem_limit_bytes=KERNEL_VMEM),
        cost_estimate=pl.CostEstimate(
            flops=2 * ranks * tokens * columns, bytes_accessed=tokens * columns * 2 + ranks * columns * 3, transcendentals=0
        ),
        name="lowrank_part",
    )(in_vmem(left), in_vmem(grad_out))


def delta_body(parts, tiles, basis_ref, *refs):
    *held, out_ref, buffer, sems = refs
    each = len(held) // parts
    wide = held[0].shape[1] // tiles
    copies = []
    for k in range(parts):
        for j in range(tiles):
            here = pl.ds(j * wide, wide)
            ranks = jnp.concatenate([piece[:, here] for piece in held[k * each : (k + 1) * each]], 0)
            there = pl.ds((k * tiles + j) * wide, wide)
            buffer[:, there] = jnp.dot(basis_ref[k], ranks, preferred_element_type=jnp.float32).astype(buffer.dtype)
            copy = pltpu.make_async_copy(buffer.at[:, there], out_ref.at[:, there], sems.at[k * tiles + j])
            copy.start()
            copies.append(copy)
    for copy in copies:
        copy.wait()


def delta_product(basis, held):
    parts, rows, ranks = basis.shape
    columns = held[0].shape[1]
    tiles = 2
    shape = (rows, parts * columns)
    whole = pl.BlockSpec(memory_space=pltpu.VMEM)
    return pl.pallas_call(
        functools.partial(delta_body, parts, tiles),
        in_specs=[whole] * (1 + len(held)),
        out_specs=pl.BlockSpec(memory_space=pl.ANY),
        out_shape=jax.ShapeDtypeStruct(shape, jnp.bfloat16),
        scratch_shapes=[pltpu.VMEM(shape, jnp.bfloat16), pltpu.SemaphoreType.DMA((parts * tiles,))],
        compiler_params=pltpu.CompilerParams(vmem_limit_bytes=KERNEL_VMEM),
        cost_estimate=pl.CostEstimate(
            flops=2 * parts * ranks * rows * columns, bytes_accessed=2 * (ranks + rows) * parts * columns, transcendentals=0
        ),
        name="delta_product",
    )(in_vmem(basis), *map(in_vmem, held))


def gathered_basis(basis):
    z, y, c = (lax.axis_index(a) for a in DP)
    odd = z % 2 == 1
    same, flipped = (lax.ppermute(basis, ALL, crossing(flip)) for flip in (0, 1))
    pair = jnp.stack([jnp.where(odd, flipped, same), jnp.where(odd, same, flipped)])
    whole = jnp.zeros((Y, *pair.shape), basis.dtype)
    whole = lax.dynamic_update_slice_in_dim(whole, pair[None], y, 0)
    for far in (1, 3, 2):
        came = lax.ppermute(pair, "y", [(i, (i + far) % Y) for i in range(Y)])
        whole = lax.dynamic_update_slice_in_dim(whole, came[None], (y + Y - far) % Y, 0)
    other = lax.ppermute(whole, "c", [(0, 1), (1, 0)])
    first = c == 0
    both = jnp.stack([jnp.where(first, whole, other), jnp.where(first, other, whole)])
    return both.transpose(2, 1, 0, 3, 4).reshape(-1, basis.shape[1])


def x_pairs(offset):
    return [(c * X + x, c * X + paired(x, X, offset + c, 1)) for c in range(C) for x in range(X)]


def exchanged(x, step):
    return lax.ppermute(x, DP, swap(step))


def joined(pieces, axis):
    return lax.optimization_barrier(jnp.concatenate(pieces, axis))


def summed_lowrank(keep, send):
    f32, bf16 = jnp.float32, jnp.bfloat16
    keep, send = list(keep), list(send)
    for at in range(len(APART[0])):
        for k, steps in enumerate(APART):
            came = exchanged(send[k], steps[at]).astype(f32)
            half = came.shape[0] // 2
            send[k] = (keep[k][half:] + came[half:]).astype(bf16)
            keep[k] = keep[k][:half] + came[:half]
    kept, sent = jnp.concatenate(keep, 1), jnp.concatenate(send, 1)
    for step in TOGETHER[:-1]:
        came = exchanged(sent, step).astype(f32)
        half = came.shape[0] // 2
        sent = (kept[half:] + came[half:]).astype(bf16)
        kept = kept[:half] + came[:half]
    return kept + exchanged(sent, TOGETHER[-1]).astype(f32)


def spread(held):
    for step in reversed(TOGETHER):
        held = joined([held, exchanged(held, step)], 0)
    columns = held.shape[1] // len(APART)
    parts = [held[:, k * columns : (k + 1) * columns] for k in range(len(APART))]
    for at in reversed(range(2, len(APART[0]))):
        parts = [joined([part, exchanged(part, steps[at])], 0) for part, steps in zip(parts, APART)]
    came = [exchanged(part, steps[1]) for part, steps in zip(parts, APART)]
    pieces = []
    for part, new, steps in zip(parts, came, APART):
        pieces += [part, new, exchanged(part, steps[0]), exchanged(new, steps[0])]
    return pieces


def on_device(features, grad_out, basis, first_moment, second_moment):
    me = place(*(lax.axis_index(a) for a in DP))
    rows = first_moment.shape[0]
    table = lax.dynamic_index_in_dim(jnp.asarray(rank_table(rows)), me, 0, keepdims=False)
    parts, ranks = table.shape
    chosen = (lax.broadcasted_iota(jnp.int32, (parts, ranks, ranks), 1) == table[:, None, :]).astype(jnp.bfloat16)
    ordered_basis = jnp.einsum("dr,krp->kdp", basis, chosen, preferred_element_type=jnp.float32).astype(jnp.bfloat16)

    met, chosen, ordered_basis = lax.optimization_barrier((gathered_basis(basis), chosen, ordered_basis))
    total = jnp.dot(features, met, preferred_element_type=jnp.float32)
    for offset in (0, 1):
        total = total + lax.ppermute(total.astype(jnp.bfloat16), ("c", "x"), x_pairs(offset)).astype(jnp.float32)
    projected = total.astype(jnp.bfloat16)
    left = jnp.einsum("krp,tr->kpt", chosen, projected, preferred_element_type=jnp.float32).astype(jnp.bfloat16)

    keep, send = zip(*(lowrank_part(left[k], grad_out, k, parts) for k in range(parts)))
    lowrank = summed_lowrank(keep, send)

    new_first = first_decay * first_moment + (1.0 - first_decay) * lowrank
    new_second = second_decay * second_moment + (1.0 - second_decay) * lowrank * lowrank
    first_fix = 1.0 - first_decay**STEP
    second_fix = 1.0 - second_decay**STEP
    normalized = (
        new_first / first_fix / (jnp.sqrt(new_second / second_fix) + epsilon_term)
    ).astype(jnp.bfloat16)
    delta = delta_product(ordered_basis, spread(normalized))
    return (delta, new_first, new_second)


def solution(mesh):
    fine = Mesh(mesh.devices.reshape(Z, Y, C, X), ALL)
    rows_columns = P(DP, "x")
    in_specs = (rows_columns, rows_columns, P(DP, None), rows_columns, rows_columns)
    return jax.shard_map(
        on_device, mesh=fine, in_specs=in_specs, out_specs=(rows_columns,) * 3, check_vma=False
    )
```

```python
import functools

import jax
import jax.numpy as jnp
import numpy as np
from jax import lax
from jax.experimental import pallas as pl
from jax.experimental.pallas import tpu as pltpu
from jax.sharding import Mesh, PartitionSpec as P

STEP = 100

first_decay = 0.9
second_decay = 0.999
epsilon_term = 1e-08

Z, Y, C, X = 8, 4, 2, 4
KERNEL_VMEM = 16 * 1024 * 1024
ALL = ("z", "y", "c", "x")
DP = ("z", "y", "c")


def place(z, y, c):
    return (z * Y + y) * C + c


def paired(i, size, offset, far):
    return (i + far) % size if (i + offset) % 2 == 0 else (i - far) % size


def partner(step, z, y, c):
    axis, offset, far = step
    half = (z + y + c) % 2
    if axis == "z":
        z = paired(z, Z, offset + half, far)
    elif axis == "y":
        y = paired(y, Y, offset + half, far)
    return z, y, 1 - c


APART = (
    (("c", 0, 0), ("y", 0, 1), ("y", 1, 1), ("z", 0, 1), ("z", 1, 1)),
    (("c", 0, 0), ("z", 0, 1), ("z", 1, 1), ("y", 0, 1), ("y", 1, 1)),
)
TOGETHER = (("z", 0, 3),)
COORDS = [(z, y, c) for z in range(Z) for y in range(Y) for c in range(C)]


def swap(step):
    return [(place(*at), place(*partner(step, *at))) for at in COORDS]


def orders(steps):
    held = {at: [place(*at)] for at in COORDS}
    for step in reversed(steps):
        held = {at: held[at] + held[partner(step, *at)] for at in COORDS}
    for blocks in held.values():
        assert sorted(blocks) == list(range(Z * Y * C))
    return np.array([held[at] for at in COORDS], np.int32)


def rank_table(rows):
    blocks = np.stack([orders(steps + TOGETHER) for steps in APART], 1)
    return (blocks[..., None] * rows + np.arange(rows, dtype=np.int32)).reshape(Z * Y * C, len(APART), -1)


def crossing(flip):
    full = lambda z, y, c, x: place(z, y, c) * X + x
    return [
        (full(2 * x + (b ^ flip), y, c, (2 * x + 2 - q) % X), full(2 * q + b, y, c, x))
        for x in range(X) for q in range(Z // 2) for b in range(2) for y in range(Y) for c in range(C)
    ]


def in_vmem(x):
    return pltpu.with_memory_space_constraint(x, pltpu.VMEM)


def lowrank_body(first, tiles, left_ref, grad_ref, keep_ref, send_ref, buffer, sems):
    half, columns = keep_ref.shape
    wide = columns // tiles

    def copy(j):
        return pltpu.make_async_copy(grad_ref.at[:, pl.ds(first + j * wide, wide)], buffer.at[j], sems.at[j])

    for j in range(tiles):
        copy(j).start()
    for j in range(tiles):
        copy(j).wait()
        product = jnp.dot(left_ref[...], buffer[j], preferred_element_type=jnp.float32)
        here = pl.ds(j * wide, wide)
        keep_ref[:, here] = product[:half]
        send_ref[:, here] = product[half:].astype(send_ref.dtype)


def lowrank_part(left, grad_out, at, parts):
    ranks, tokens = left.shape
    columns = grad_out.shape[1] // parts
    tiles = 4
    whole = pl.BlockSpec(memory_space=pltpu.VMEM)
    return pl.pallas_call(
        functools.partial(lowrank_body, at * columns, tiles),
        in_specs=[whole, pl.BlockSpec(memory_space=pl.ANY)],
        out_specs=[whole] * 2,
        out_shape=[pltpu.VMEM((ranks // 2, columns), jnp.float32), pltpu.VMEM((ranks // 2, columns), jnp.bfloat16)],
        scratch_shapes=[pltpu.VMEM((tiles, tokens, columns // tiles), grad_out.dtype), pltpu.SemaphoreType.DMA((tiles,))],
        compiler_params=pltpu.CompilerParams(vmem_limit_bytes=KERNEL_VMEM),
        cost_estimate=pl.CostEstimate(
            flops=2 * ranks * tokens * columns, bytes_accessed=tokens * columns * 2 + ranks * columns * 3, transcendentals=0
        ),
        name="lowrank_part",
    )(in_vmem(left), pltpu.with_memory_space_constraint(grad_out, pltpu.HBM))


def delta_body(parts, tiles, basis_ref, *refs):
    *held, out_ref, buffer, sems = refs
    each = len(held) // parts
    wide = held[0].shape[1] // tiles
    copies = []
    for k in range(parts):
        for j in range(tiles):
            here = pl.ds(j * wide, wide)
            ranks = jnp.concatenate([piece[:, here] for piece in held[k * each : (k + 1) * each]], 0)
            there = pl.ds((k * tiles + j) * wide, wide)
            buffer[:, there] = jnp.dot(basis_ref[k], ranks, preferred_element_type=jnp.float32).astype(buffer.dtype)
            copy = pltpu.make_async_copy(buffer.at[:, there], out_ref.at[:, there], sems.at[k * tiles + j])
            copy.start()
            copies.append(copy)
    for copy in copies:
        copy.wait()


def delta_product(basis, held):
    parts, rows, ranks = basis.shape
    columns = held[0].shape[1]
    tiles = 2
    shape = (rows, parts * columns)
    whole = pl.BlockSpec(memory_space=pltpu.VMEM)
    return pl.pallas_call(
        functools.partial(delta_body, parts, tiles),
        in_specs=[whole] * (1 + len(held)),
        out_specs=pl.BlockSpec(memory_space=pl.ANY),
        out_shape=jax.ShapeDtypeStruct(shape, jnp.bfloat16),
        scratch_shapes=[pltpu.VMEM(shape, jnp.bfloat16), pltpu.SemaphoreType.DMA((parts * tiles,))],
        compiler_params=pltpu.CompilerParams(vmem_limit_bytes=KERNEL_VMEM),
        cost_estimate=pl.CostEstimate(
            flops=2 * parts * ranks * rows * columns, bytes_accessed=2 * (ranks + rows) * parts * columns, transcendentals=0
        ),
        name="delta_product",
    )(in_vmem(basis), *map(in_vmem, held))


def gathered_basis(basis):
    z, y, c = (lax.axis_index(a) for a in DP)
    odd = z % 2 == 1
    same, flipped = (lax.ppermute(basis, ALL, crossing(flip)) for flip in (0, 1))
    pair = jnp.stack([jnp.where(odd, flipped, same), jnp.where(odd, same, flipped)])
    pieces = [pair]
    for far in (1, 3, 2):
        to = [((i * C + k), (i + far) % Y * C + (k + far) % C) for i in range(Y) for k in range(C)]
        pieces.append(lax.ppermute(pair, ("y", "c"), to))
    own = jnp.stack(pieces)
    other = lax.ppermute(own, "c", [(0, 1), (1, 0)])
    whole = jnp.zeros((2, Y, C, *basis.shape), basis.dtype)
    for core, some in ((c, own), (1 - c, other)):
        for at, far in enumerate((0, 1, 3, 2)):
            place_at = (0, (y + Y - far) % Y, (core + far) % C, 0, 0)
            whole = lax.dynamic_update_slice(whole, some[at][:, None, None], place_at)
    return whole.reshape(-1, basis.shape[1])


def x_pairs(offset):
    return [(c * X + x, c * X + paired(x, X, offset + c, 1)) for c in range(C) for x in range(X)]


def exchanged(x, step):
    return lax.ppermute(x, DP, swap(step))


def joined(pieces, axis):
    return lax.optimization_barrier(jnp.concatenate(pieces, axis))


def summed_lowrank(keep, send):
    f32, bf16 = jnp.float32, jnp.bfloat16
    keep, send = list(keep), list(send)
    for at in range(len(APART[0])):
        for k, steps in enumerate(APART):
            came = exchanged(send[k], steps[at])
            half = came.shape[0] // 2
            send[k] = (keep[k][half:] + came[half:].astype(f32)).astype(bf16)
            keep[k] = keep[k][:half] + came[:half].astype(f32)
    kept, sent = jnp.concatenate(keep, 1), jnp.concatenate(send, 1)
    for step in TOGETHER[:-1]:
        came = exchanged(sent, step).astype(f32)
        half = came.shape[0] // 2
        sent = (kept[half:] + came[half:]).astype(bf16)
        kept = kept[:half] + came[:half]
    return kept + exchanged(sent, TOGETHER[-1]).astype(f32)


def spread(held):
    for step in reversed(TOGETHER):
        held = joined([held, exchanged(held, step)], 0)
    columns = held.shape[1] // len(APART)
    parts = [held[:, k * columns : (k + 1) * columns] for k in range(len(APART))]
    for at in reversed(range(2, len(APART[0]))):
        parts = [joined([part, exchanged(part, steps[at])], 0) for part, steps in zip(parts, APART)]
    came = [exchanged(part, steps[1]) for part, steps in zip(parts, APART)]
    pieces = []
    for part, new, steps in zip(parts, came, APART):
        pieces += [part, new, exchanged(part, steps[0]), exchanged(new, steps[0])]
    return pieces


def on_device(features, grad_out, basis, first_moment, second_moment):
    me = place(*(lax.axis_index(a) for a in DP))
    rows = first_moment.shape[0]
    table = lax.dynamic_index_in_dim(jnp.asarray(rank_table(rows)), me, 0, keepdims=False)
    parts, ranks = table.shape
    chosen = (lax.broadcasted_iota(jnp.int32, (parts, ranks, ranks), 1) == table[:, None, :]).astype(jnp.bfloat16)
    ordered_basis = jnp.einsum("dr,krp->kdp", basis, chosen, preferred_element_type=jnp.float32).astype(jnp.bfloat16)

    met, chosen, ordered_basis = lax.optimization_barrier((gathered_basis(basis), chosen, ordered_basis))
    total = jnp.dot(features, met, preferred_element_type=jnp.float32)
    for offset in (0, 1):
        total = total + lax.ppermute(total.astype(jnp.bfloat16), ("c", "x"), x_pairs(offset)).astype(jnp.float32)
    projected = total.astype(jnp.bfloat16)
    left = jnp.einsum("krp,tr->kpt", chosen, projected, preferred_element_type=jnp.float32).astype(jnp.bfloat16)

    keep, send = zip(*(lowrank_part(left[k], grad_out, k, parts) for k in range(parts)))
    lowrank = summed_lowrank(keep, send)

    new_first = first_decay * first_moment + (1.0 - first_decay) * lowrank
    new_second = second_decay * second_moment + (1.0 - second_decay) * lowrank * lowrank
    first_fix = 1.0 - first_decay**STEP
    second_fix = 1.0 - second_decay**STEP
    normalized = (
        new_first / first_fix / (jnp.sqrt(new_second / second_fix) + epsilon_term)
    ).astype(jnp.bfloat16)
    delta = delta_product(ordered_basis, spread(normalized))
    return (delta, new_first, new_second)


def solution(mesh):
    fine = Mesh(mesh.devices.reshape(Z, Y, C, X), ALL)
    rows_columns = P(DP, "x")
    in_specs = (rows_columns, rows_columns, P(DP, None), rows_columns, rows_columns)
    return jax.shard_map(
        on_device, mesh=fine, in_specs=in_specs, out_specs=(rows_columns,) * 3, check_vma=False
    )
```

```python
import functools

import jax
import jax.numpy as jnp
import numpy as np
from jax import lax
from jax.experimental import pallas as pl
from jax.experimental.pallas import tpu as pltpu
from jax.sharding import Mesh, PartitionSpec as P

STEP = 100

first_decay = 0.9
second_decay = 0.999
epsilon_term = 1e-08

Z, Y, C, X = 8, 4, 2, 4
KERNEL_VMEM = 16 * 1024 * 1024
ALL = ("z", "y", "c", "x")
DP = ("z", "y", "c")


def place(z, y, c):
    return (z * Y + y) * C + c


def paired(i, size, offset, far):
    return (i + far) % size if (i + offset) % 2 == 0 else (i - far) % size


def partner(step, z, y, c):
    axis, offset, far = step
    half = (z + y + c) % 2
    if axis == "z":
        z = paired(z, Z, offset + half, far)
    elif axis == "y":
        y = paired(y, Y, offset + half, far)
    return z, y, 1 - c


HALVING = (
    (("c", 0, 0), ("y", 0, 1), ("y", 1, 1), ("z", 0, 1), ("z", 1, 1)),
    (("c", 0, 0), ("z", 0, 1), ("z", 1, 1), ("y", 0, 1), ("y", 1, 1)),
)
LAST = ("z", 0, 3)
COORDS = [(z, y, c) for z in range(Z) for y in range(Y) for c in range(C)]


def swap(step):
    return [(place(*at), place(*partner(step, *at))) for at in COORDS]


def orders(steps):
    held = {at: [place(*at)] for at in COORDS}
    for step in reversed(steps):
        held = {at: held[at] + held[partner(step, *at)] for at in COORDS}
    for blocks in held.values():
        assert sorted(blocks) == list(range(Z * Y * C))
    return np.array([held[at] for at in COORDS], np.int32)


def rank_table(rows):
    blocks = np.stack([orders((*steps, LAST)) for steps in HALVING], 1)
    return (blocks[..., None] * rows + np.arange(rows, dtype=np.int32)).reshape(Z * Y * C, len(HALVING), -1)


def crossing(flip):
    full = lambda z, y, c, x: place(z, y, c) * X + x
    return [
        (full(2 * x + (b ^ flip), y, c, (2 * x + 2 - q) % X), full(2 * q + b, y, c, x))
        for x in range(X) for q in range(Z // 2) for b in range(2) for y in range(Y) for c in range(C)
    ]


def in_vmem(x):
    return pltpu.with_memory_space_constraint(x, pltpu.VMEM)


def staged_body(from_ref, to_ref, sem):
    copy = pltpu.make_async_copy(from_ref, to_ref, sem)
    copy.start()
    copy.wait()


def staged(x):
    return pl.pallas_call(
        staged_body,
        in_specs=[pl.BlockSpec(memory_space=pl.ANY)],
        out_specs=pl.BlockSpec(memory_space=pl.ANY),
        out_shape=pltpu.VMEM(x.shape, x.dtype),
        scratch_shapes=[pltpu.SemaphoreType.DMA],
        compiler_params=pltpu.CompilerParams(vmem_limit_bytes=KERNEL_VMEM),
        cost_estimate=pl.CostEstimate(flops=0, bytes_accessed=2 * x.size * x.dtype.itemsize, transcendentals=0),
        name="staged",
    )(pltpu.with_memory_space_constraint(x, pltpu.HBM))


def lowrank_body(first, tiles, left_ref, grad_ref, keep_ref, send_ref):
    half, columns = keep_ref.shape
    wide = columns // tiles
    for j in range(tiles):
        product = jnp.dot(left_ref[...], grad_ref[:, pl.ds(first + j * wide, wide)], preferred_element_type=jnp.float32)
        here = pl.ds(j * wide, wide)
        keep_ref[:, here] = product[:half]
        send_ref[:, here] = product[half:].astype(send_ref.dtype)


def lowrank_part(left, grad_out, at, parts):
    ranks, tokens = left.shape
    columns = grad_out.shape[1] // parts
    whole = pl.BlockSpec(memory_space=pltpu.VMEM)
    return pl.pallas_call(
        functools.partial(lowrank_body, at * columns, 4),
        in_specs=[whole] * 2,
        out_specs=[whole] * 2,
        out_shape=[pltpu.VMEM((ranks // 2, columns), jnp.float32), pltpu.VMEM((ranks // 2, columns), jnp.bfloat16)],
        compiler_params=pltpu.CompilerParams(vmem_limit_bytes=KERNEL_VMEM),
        cost_estimate=pl.CostEstimate(
            flops=2 * ranks * tokens * columns, bytes_accessed=tokens * columns * 2 + ranks * columns * 3, transcendentals=0
        ),
        name="lowrank_part",
    )(in_vmem(left), in_vmem(grad_out))


def delta_body(parts, tiles, basis_ref, *refs):
    *held, out_ref, buffer, sems = refs
    each = len(held) // parts
    wide = held[0].shape[1] // tiles
    copies = []
    for k in range(parts):
        for j in range(tiles):
            here = pl.ds(j * wide, wide)
            ranks = jnp.concatenate([piece[:, here] for piece in held[k * each : (k + 1) * each]], 0)
            there = pl.ds((k * tiles + j) * wide, wide)
            buffer[:, there] = jnp.dot(basis_ref[k], ranks, preferred_element_type=jnp.float32).astype(buffer.dtype)
            copy = pltpu.make_async_copy(buffer.at[:, there], out_ref.at[:, there], sems.at[k * tiles + j])
            copy.start()
            copies.append(copy)
    for copy in copies:
        copy.wait()


def delta_product(basis, held):
    parts, rows, ranks = basis.shape
    columns = held[0].shape[1]
    tiles = 2
    shape = (rows, parts * columns)
    whole = pl.BlockSpec(memory_space=pltpu.VMEM)
    return pl.pallas_call(
        functools.partial(delta_body, parts, tiles),
        in_specs=[whole] * (1 + len(held)),
        out_specs=pl.BlockSpec(memory_space=pl.ANY),
        out_shape=jax.ShapeDtypeStruct(shape, jnp.bfloat16),
        scratch_shapes=[pltpu.VMEM(shape, jnp.bfloat16), pltpu.SemaphoreType.DMA((parts * tiles,))],
        compiler_params=pltpu.CompilerParams(vmem_limit_bytes=KERNEL_VMEM),
        cost_estimate=pl.CostEstimate(
            flops=2 * parts * ranks * rows * columns, bytes_accessed=2 * (ranks + rows) * parts * columns, transcendentals=0
        ),
        name="delta_product",
    )(in_vmem(basis), *map(in_vmem, held))


def gathered_basis(basis):
    z, y, c = (lax.axis_index(a) for a in DP)
    odd = z % 2 == 1
    same, flipped = (lax.ppermute(basis, ALL, crossing(flip)) for flip in (0, 1))
    pair = jnp.stack([jnp.where(odd, flipped, same), jnp.where(odd, same, flipped)])
    pieces = [pair]
    for far in (1, 3, 2):
        to = [((i * C + k), (i + far) % Y * C + (k + far) % C) for i in range(Y) for k in range(C)]
        pieces.append(lax.ppermute(pair, ("y", "c"), to))
    own = jnp.stack(pieces)
    other = lax.ppermute(own, "c", [(0, 1), (1, 0)])
    whole = jnp.zeros((2, Y, C, *basis.shape), basis.dtype)
    for core, some in ((c, own), (1 - c, other)):
        for at, far in enumerate((0, 1, 3, 2)):
            place_at = (0, (y + Y - far) % Y, (core + far) % C, 0, 0)
            whole = lax.dynamic_update_slice(whole, some[at][:, None, None], place_at)
    return whole.reshape(-1, basis.shape[1])


def x_pairs(offset):
    return [(c * X + x, c * X + paired(x, X, offset + c, 1)) for c in range(C) for x in range(X)]


def exchanged(x, step):
    return lax.ppermute(x, DP, swap(step))


def joined(pieces, axis):
    return lax.optimization_barrier(jnp.concatenate(pieces, axis))


def shared_lowrank(keep, send):
    f32, bf16 = jnp.float32, jnp.bfloat16
    keep, send = list(keep), list(send)
    steps_left = len(HALVING[0])
    for at in range(steps_left):
        for k, steps in enumerate(HALVING):
            came = exchanged(send[k], steps[at])
            half = came.shape[0] // 2
            if at + 1 < steps_left:
                send[k] = (keep[k][half:] + came[half:].astype(f32)).astype(bf16)
                keep[k] = keep[k][:half] + came[:half].astype(f32)
            else:
                keep[k] = keep[k] + came.astype(f32)
    return keep


def update_body(parts, came_ref, own_ref, other_ref, *refs):
    kept, outs = refs[:parts], refs[parts:]
    first_ref, second_ref, *normalized = outs
    rows, columns = first_ref.shape
    first_fix = 1.0 - first_decay**STEP
    second_fix = 1.0 - second_decay**STEP
    wide = columns // parts
    for k in range(parts):
        here = pl.ds(k * wide, wide)
        came = came_ref[:, here].astype(jnp.float32)
        held = kept[k][...]
        values = []
        for at, moments in enumerate((own_ref, other_ref)):
            there = 1 - at
            lowrank = held[at * rows : (at + 1) * rows] + came[there * rows : (there + 1) * rows]
            new_first = first_decay * moments[0, :, here] + (1.0 - first_decay) * lowrank
            new_second = second_decay * moments[1, :, here] + (1.0 - second_decay) * lowrank * lowrank
            values.append(new_first / first_fix / (jnp.sqrt(new_second / second_fix) + epsilon_term))
            if at == 0:
                first_ref[:, here] = new_first
                second_ref[:, here] = new_second
        normalized[k][...] = jnp.concatenate(values, 0).astype(jnp.bfloat16)


def updated(kept, came, own, other):
    shape = own.shape[1:]
    whole = pl.BlockSpec(memory_space=pltpu.VMEM)
    return pl.pallas_call(
        functools.partial(update_body, len(kept)),
        in_specs=[whole] * (3 + len(kept)),
        out_specs=[whole] * (2 + len(kept)),
        out_shape=[
            *[jax.ShapeDtypeStruct(shape, jnp.float32)] * 2,
            *(pltpu.VMEM(part.shape, jnp.bfloat16) for part in kept),
        ],
        compiler_params=pltpu.CompilerParams(vmem_limit_bytes=KERNEL_VMEM),
        cost_estimate=pl.CostEstimate(flops=60 * own.size, bytes_accessed=20 * own.size, transcendentals=own.size),
        name="updated",
    )(in_vmem(came), in_vmem(own), in_vmem(other), *map(in_vmem, kept))


def spread(parts):
    for at in reversed(range(2, len(HALVING[0]))):
        parts = [joined([part, exchanged(part, steps[at])], 0) for part, steps in zip(parts, HALVING)]
    came = [exchanged(part, steps[1]) for part, steps in zip(parts, HALVING)]
    pieces = []
    for part, new, steps in zip(parts, came, HALVING):
        pieces += [part, new, exchanged(part, steps[0]), exchanged(new, steps[0])]
    return pieces


def on_device(features, grad_out, basis, first_moment, second_moment):
    me = place(*(lax.axis_index(a) for a in DP))
    rows = first_moment.shape[0]
    table = lax.dynamic_index_in_dim(jnp.asarray(rank_table(rows)), me, 0, keepdims=False)
    parts, ranks = table.shape
    chosen = (lax.broadcasted_iota(jnp.int32, (parts, ranks, ranks), 1) == table[:, None, :]).astype(jnp.bfloat16)
    ordered_basis = jnp.einsum("dr,krp->kdp", basis, chosen, preferred_element_type=jnp.float32).astype(jnp.bfloat16)

    met, chosen, ordered_basis = lax.optimization_barrier((gathered_basis(basis), chosen, ordered_basis))
    total = jnp.dot(features, met, preferred_element_type=jnp.float32)
    sent, *both = lax.optimization_barrier((total.astype(jnp.bfloat16), first_moment, second_moment))
    total = total + lax.ppermute(sent, ("c", "x"), x_pairs(0)).astype(jnp.float32)
    moments = jnp.stack(both)
    sent, grad_out = lax.optimization_barrier((total.astype(jnp.bfloat16), grad_out))
    total = total + lax.ppermute(sent, ("c", "x"), x_pairs(1)).astype(jnp.float32)
    projected, grad_out = lax.optimization_barrier((total.astype(jnp.bfloat16), staged(grad_out)))
    other_moments = exchanged(moments, LAST)
    left = jnp.einsum("krp,tr->kpt", chosen, projected, preferred_element_type=jnp.float32).astype(jnp.bfloat16)

    keep, send = zip(*(lowrank_part(left[k], grad_out, k, parts) for k in range(parts)))

    send, other_moments = lax.optimization_barrier((send, other_moments))
    kept = shared_lowrank(keep, send)
    came = exchanged(jnp.concatenate([part.astype(jnp.bfloat16) for part in kept], 1), LAST)
    new_first, new_second, *normalized = updated(kept, came, moments, other_moments)
    delta = delta_product(ordered_basis, spread(normalized))
    return (delta, new_first, new_second)


def solution(mesh):
    fine = Mesh(mesh.devices.reshape(Z, Y, C, X), ALL)
    rows_columns = P(DP, "x")
    in_specs = (rows_columns, rows_columns, P(DP, None), rows_columns, rows_columns)
    return jax.shard_map(
        on_device, mesh=fine, in_specs=in_specs, out_specs=(rows_columns,) * 3, check_vma=False
    )
```

```python
import functools

import jax
import jax.numpy as jnp
import numpy as np
from jax import lax
from jax.experimental import pallas as pl
from jax.experimental.pallas import tpu as pltpu
from jax.sharding import Mesh, PartitionSpec as P

STEP = 100

first_decay = 0.9
second_decay = 0.999
epsilon_term = 1e-08

Z, Y, C, X = 8, 4, 2, 4
KERNEL_VMEM = 16 * 1024 * 1024
ALL = ("z", "y", "c", "x")
DP = ("z", "y", "c")


def place(z, y, c):
    return (z * Y + y) * C + c


def paired(i, size, offset, far):
    return (i + far) % size if (i + offset) % 2 == 0 else (i - far) % size


def partner(step, z, y, c):
    axis, offset, far = step
    half = (z + y + c) % 2
    if axis == "z":
        z = paired(z, Z, offset + half, far)
    elif axis == "y":
        y = paired(y, Y, offset + half, far)
    return z, y, 1 - c


HALVING = (
    (("c", 0, 0), ("y", 0, 1), ("y", 1, 1), ("z", 0, 1), ("z", 1, 1)),
    (("c", 0, 0), ("z", 0, 1), ("z", 1, 1), ("y", 0, 1), ("y", 1, 1)),
)
LAST = ("z", 0, 3)
COORDS = [(z, y, c) for z in range(Z) for y in range(Y) for c in range(C)]


def swap(step):
    return [(place(*at), place(*partner(step, *at))) for at in COORDS]


def orders(steps):
    held = {at: [place(*at)] for at in COORDS}
    for step in reversed(steps):
        held = {at: held[at] + held[partner(step, *at)] for at in COORDS}
    for blocks in held.values():
        assert sorted(blocks) == list(range(Z * Y * C))
    return np.array([held[at] for at in COORDS], np.int32)


def rank_table(rows):
    blocks = np.stack([orders((*steps, LAST)) for steps in HALVING], 1)
    return (blocks[..., None] * rows + np.arange(rows, dtype=np.int32)).reshape(Z * Y * C, len(HALVING), -1)


def crossing(flip):
    full = lambda z, y, c, x: place(z, y, c) * X + x
    return [
        (full(2 * x + (b ^ flip), y, c, (2 * x + 2 - q) % X), full(2 * q + b, y, c, x))
        for x in range(X) for q in range(Z // 2) for b in range(2) for y in range(Y) for c in range(C)
    ]


def in_vmem(x):
    return pltpu.with_memory_space_constraint(x, pltpu.VMEM)


def staged_body(from_ref, to_ref, sem):
    copy = pltpu.make_async_copy(from_ref, to_ref, sem)
    copy.start()
    copy.wait()


def staged(x):
    return pl.pallas_call(
        staged_body,
        in_specs=[pl.BlockSpec(memory_space=pl.ANY)],
        out_specs=pl.BlockSpec(memory_space=pl.ANY),
        out_shape=pltpu.VMEM(x.shape, x.dtype),
        scratch_shapes=[pltpu.SemaphoreType.DMA],
        compiler_params=pltpu.CompilerParams(vmem_limit_bytes=KERNEL_VMEM),
        cost_estimate=pl.CostEstimate(flops=0, bytes_accessed=2 * x.size * x.dtype.itemsize, transcendentals=0),
        name="staged",
    )(pltpu.with_memory_space_constraint(x, pltpu.HBM))


def lowrank_body(first, tiles, left_ref, grad_ref, keep_ref, send_ref):
    half, columns = keep_ref.shape
    wide = columns // tiles
    for j in range(tiles):
        product = jnp.dot(left_ref[...], grad_ref[:, pl.ds(first + j * wide, wide)], preferred_element_type=jnp.float32)
        here = pl.ds(j * wide, wide)
        keep_ref[:, here] = product[:half]
        send_ref[:, here] = product[half:].astype(send_ref.dtype)


def lowrank_part(left, grad_out, at, parts):
    ranks, tokens = left.shape
    columns = grad_out.shape[1] // parts
    whole = pl.BlockSpec(memory_space=pltpu.VMEM)
    return pl.pallas_call(
        functools.partial(lowrank_body, at * columns, 4),
        in_specs=[whole] * 2,
        out_specs=[whole] * 2,
        out_shape=[pltpu.VMEM((ranks // 2, columns), jnp.float32), pltpu.VMEM((ranks // 2, columns), jnp.bfloat16)],
        compiler_params=pltpu.CompilerParams(vmem_limit_bytes=KERNEL_VMEM),
        cost_estimate=pl.CostEstimate(
            flops=2 * ranks * tokens * columns, bytes_accessed=tokens * columns * 2 + ranks * columns * 3, transcendentals=0
        ),
        name="lowrank_part",
    )(in_vmem(left), in_vmem(grad_out))


def delta_body(parts, tiles, basis_ref, *refs):
    *held, out_ref, buffer, sems = refs
    each = len(held) // parts
    wide = held[0].shape[1] // tiles
    copies = []
    for k in range(parts):
        for j in range(tiles):
            here = pl.ds(j * wide, wide)
            ranks = jnp.concatenate([piece[:, here] for piece in held[k * each : (k + 1) * each]], 0)
            there = pl.ds((k * tiles + j) * wide, wide)
            buffer[:, there] = jnp.dot(basis_ref[k], ranks, preferred_element_type=jnp.float32).astype(buffer.dtype)
            copy = pltpu.make_async_copy(buffer.at[:, there], out_ref.at[:, there], sems.at[k * tiles + j])
            copy.start()
            copies.append(copy)
    for copy in copies:
        copy.wait()


def delta_product(basis, held):
    parts, rows, ranks = basis.shape
    columns = held[0].shape[1]
    tiles = 2
    shape = (rows, parts * columns)
    whole = pl.BlockSpec(memory_space=pltpu.VMEM)
    return pl.pallas_call(
        functools.partial(delta_body, parts, tiles),
        in_specs=[whole] * (1 + len(held)),
        out_specs=pl.BlockSpec(memory_space=pl.ANY),
        out_shape=jax.ShapeDtypeStruct(shape, jnp.bfloat16),
        scratch_shapes=[pltpu.VMEM(shape, jnp.bfloat16), pltpu.SemaphoreType.DMA((parts * tiles,))],
        compiler_params=pltpu.CompilerParams(vmem_limit_bytes=KERNEL_VMEM),
        cost_estimate=pl.CostEstimate(
            flops=2 * parts * ranks * rows * columns, bytes_accessed=2 * (ranks + rows) * parts * columns, transcendentals=0
        ),
        name="delta_product",
    )(in_vmem(basis), *map(in_vmem, held))


def gathered_basis(basis):
    z, y, c = (lax.axis_index(a) for a in DP)
    odd = z % 2 == 1
    same, flipped = (lax.ppermute(basis, ALL, crossing(flip)) for flip in (0, 1))
    pair = jnp.stack([jnp.where(odd, flipped, same), jnp.where(odd, same, flipped)])
    pieces = [pair]
    for far in (1, 3, 2):
        to = [((i * C + k), (i + far) % Y * C + (k + far) % C) for i in range(Y) for k in range(C)]
        pieces.append(lax.ppermute(pair, ("y", "c"), to))
    own = jnp.stack(pieces)
    other = lax.ppermute(own, "c", [(0, 1), (1, 0)])
    whole = jnp.zeros((2, Y, C, *basis.shape), basis.dtype)
    for core, some in ((c, own), (1 - c, other)):
        for at, far in enumerate((0, 1, 3, 2)):
            place_at = (0, (y + Y - far) % Y, (core + far) % C, 0, 0)
            whole = lax.dynamic_update_slice(whole, some[at][:, None, None], place_at)
    return whole.reshape(-1, basis.shape[1])


def x_pairs(offset):
    return [(c * X + x, c * X + paired(x, X, offset + c, 1)) for c in range(C) for x in range(X)]


def exchanged(x, step):
    return lax.ppermute(x, DP, swap(step))


def joined(pieces, axis):
    return lax.optimization_barrier(jnp.concatenate(pieces, axis))


def shared_lowrank(keep, send):
    f32, bf16 = jnp.float32, jnp.bfloat16
    keep, send = list(keep), list(send)
    steps_left = len(HALVING[0])
    for at in range(steps_left):
        for k, steps in enumerate(HALVING):
            came = exchanged(send[k], steps[at])
            half = came.shape[0] // 2
            if at + 1 < steps_left:
                send[k] = (keep[k][half:] + came[half:].astype(f32)).astype(bf16)
                keep[k] = keep[k][:half] + came[:half].astype(f32)
            else:
                keep[k] = keep[k] + came.astype(f32)
    return keep


def update_body(parts, came_ref, own_ref, other_ref, *refs):
    kept, outs = refs[:parts], refs[parts:]
    first_ref, second_ref, *normalized = outs
    rows, columns = first_ref.shape
    first_fix = 1.0 - first_decay**STEP
    second_fix = 1.0 - second_decay**STEP
    wide = columns // parts
    for k in range(parts):
        here = pl.ds(k * wide, wide)
        came = came_ref[:, here].astype(jnp.float32)
        held = kept[k][...]
        values = []
        for at, moments in enumerate((own_ref, other_ref)):
            there = 1 - at
            lowrank = held[at * rows : (at + 1) * rows] + came[there * rows : (there + 1) * rows]
            new_first = first_decay * moments[0, :, here] + (1.0 - first_decay) * lowrank
            new_second = second_decay * moments[1, :, here] + (1.0 - second_decay) * lowrank * lowrank
            values.append(new_first / first_fix / (jnp.sqrt(new_second / second_fix) + epsilon_term))
            if at == 0:
                first_ref[:, here] = new_first
                second_ref[:, here] = new_second
        normalized[k][...] = jnp.concatenate(values, 0).astype(jnp.bfloat16)


def updated(kept, came, own, other):
    shape = own.shape[1:]
    whole = pl.BlockSpec(memory_space=pltpu.VMEM)
    return pl.pallas_call(
        functools.partial(update_body, len(kept)),
        in_specs=[whole] * (3 + len(kept)),
        out_specs=[whole] * (2 + len(kept)),
        out_shape=[
            *[jax.ShapeDtypeStruct(shape, jnp.float32)] * 2,
            *(pltpu.VMEM(part.shape, jnp.bfloat16) for part in kept),
        ],
        compiler_params=pltpu.CompilerParams(vmem_limit_bytes=KERNEL_VMEM),
        cost_estimate=pl.CostEstimate(flops=60 * own.size, bytes_accessed=20 * own.size, transcendentals=own.size),
        name="updated",
    )(in_vmem(came), in_vmem(own), in_vmem(other), *map(in_vmem, kept))


def spread(parts):
    for at in reversed(range(2, len(HALVING[0]))):
        parts = [joined([part, exchanged(part, steps[at])], 0) for part, steps in zip(parts, HALVING)]
    came = [exchanged(part, steps[1]) for part, steps in zip(parts, HALVING)]
    pieces = []
    for part, new, steps in zip(parts, came, HALVING):
        pieces += [part, new, exchanged(part, steps[0]), exchanged(new, steps[0])]
    return pieces


def on_device(features, grad_out, basis, first_moment, second_moment):
    me = place(*(lax.axis_index(a) for a in DP))
    rows = first_moment.shape[0]
    table = lax.dynamic_index_in_dim(jnp.asarray(rank_table(rows)), me, 0, keepdims=False)
    parts, ranks = table.shape
    chosen = (lax.broadcasted_iota(jnp.int32, (parts, ranks, ranks), 1) == table[:, None, :]).astype(jnp.bfloat16)
    ordered_basis = jnp.einsum("dr,krp->kdp", basis, chosen, preferred_element_type=jnp.float32).astype(jnp.bfloat16)

    met, chosen, ordered_basis = lax.optimization_barrier((gathered_basis(basis), chosen, ordered_basis))
    total = jnp.dot(features, met, preferred_element_type=jnp.float32)
    sent, grad_out, *both = lax.optimization_barrier((total.astype(jnp.bfloat16), grad_out, first_moment, second_moment))
    total = total + lax.ppermute(sent, ("c", "x"), x_pairs(0)).astype(jnp.float32)
    moments = jnp.stack(both)
    sent, grad_out = lax.optimization_barrier((total.astype(jnp.bfloat16), staged(grad_out)))
    total = total + lax.ppermute(sent, ("c", "x"), x_pairs(1)).astype(jnp.float32)
    projected = total.astype(jnp.bfloat16)
    other_moments = exchanged(moments.astype(jnp.float16), LAST)
    left = jnp.einsum("krp,tr->kpt", chosen, projected, preferred_element_type=jnp.float32).astype(jnp.bfloat16)

    keep, send = zip(*(lowrank_part(left[k], grad_out, k, parts) for k in range(parts)))

    send, other_moments = lax.optimization_barrier((send, other_moments))
    other_moments = other_moments.astype(jnp.float32)
    kept = shared_lowrank(keep, send)
    came = exchanged(jnp.concatenate([part.astype(jnp.bfloat16) for part in kept], 1), LAST)
    new_first, new_second, *normalized = updated(kept, came, moments, other_moments)
    delta = delta_product(ordered_basis, spread(normalized))
    return (delta, new_first, new_second)


def solution(mesh):
    fine = Mesh(mesh.devices.reshape(Z, Y, C, X), ALL)
    rows_columns = P(DP, "x")
    in_specs = (rows_columns, rows_columns, P(DP, None), rows_columns, rows_columns)
    return jax.shard_map(
        on_device, mesh=fine, in_specs=in_specs, out_specs=(rows_columns,) * 3, check_vma=False
    )
```

```python
import functools

import jax
import jax.numpy as jnp
import numpy as np
from jax import lax
from jax.experimental import pallas as pl
from jax.experimental.pallas import tpu as pltpu
from jax.sharding import Mesh, PartitionSpec as P

STEP = 100

first_decay = 0.9
second_decay = 0.999
epsilon_term = 1e-08

Z, Y, C, X = 8, 4, 2, 4
KERNEL_VMEM = 16 * 1024 * 1024
ALL = ("z", "y", "c", "x")
DP = ("z", "y", "c")


def place(z, y, c):
    return (z * Y + y) * C + c


def paired(i, size, offset, far):
    return (i + far) % size if (i + offset) % 2 == 0 else (i - far) % size


def partner(step, z, y, c):
    axis, offset, far = step
    half = (z + y + c) % 2
    if axis == "z":
        z = paired(z, Z, offset + half, far)
    elif axis == "y":
        y = paired(y, Y, offset + half, far)
    return z, y, 1 - c


HALVING = (
    (("c", 0, 0), ("y", 0, 1), ("y", 1, 1), ("z", 0, 1), ("z", 1, 1)),
    (("c", 0, 0), ("z", 0, 1), ("z", 1, 1), ("y", 0, 1), ("y", 1, 1)),
)
LAST = ("z", 0, 3)
COORDS = [(z, y, c) for z in range(Z) for y in range(Y) for c in range(C)]


def swap(step):
    return [(place(*at), place(*partner(step, *at))) for at in COORDS]


def orders(steps):
    held = {at: [place(*at)] for at in COORDS}
    for step in reversed(steps):
        held = {at: held[at] + held[partner(step, *at)] for at in COORDS}
    for blocks in held.values():
        assert sorted(blocks) == list(range(Z * Y * C))
    return np.array([held[at] for at in COORDS], np.int32)


def rank_table(rows):
    blocks = np.stack([orders((*steps, LAST)) for steps in HALVING], 1)
    return (blocks[..., None] * rows + np.arange(rows, dtype=np.int32)).reshape(Z * Y * C, len(HALVING), -1)


def crossing(flip):
    full = lambda z, y, c, x: place(z, y, c) * X + x
    return [
        (full(2 * x + (b ^ flip), y, c, (2 * x + 2 - q) % X), full(2 * q + b, y, c, x))
        for x in range(X) for q in range(Z // 2) for b in range(2) for y in range(Y) for c in range(C)
    ]


def in_vmem(x):
    return pltpu.with_memory_space_constraint(x, pltpu.VMEM)


def staged_body(from_ref, to_ref, sem):
    copy = pltpu.make_async_copy(from_ref, to_ref, sem)
    copy.start()
    copy.wait()


def staged(x):
    return pl.pallas_call(
        staged_body,
        in_specs=[pl.BlockSpec(memory_space=pl.ANY)],
        out_specs=pl.BlockSpec(memory_space=pl.ANY),
        out_shape=pltpu.VMEM(x.shape, x.dtype),
        scratch_shapes=[pltpu.SemaphoreType.DMA],
        compiler_params=pltpu.CompilerParams(vmem_limit_bytes=KERNEL_VMEM),
        cost_estimate=pl.CostEstimate(flops=0, bytes_accessed=2 * x.size * x.dtype.itemsize, transcendentals=0),
        name="staged",
    )(pltpu.with_memory_space_constraint(x, pltpu.HBM))


def lowrank_body(first, tiles, left_ref, grad_ref, keep_ref, send_ref):
    half, columns = keep_ref.shape
    wide = columns // tiles
    for j in range(tiles):
        product = jnp.dot(left_ref[...], grad_ref[:, pl.ds(first + j * wide, wide)], preferred_element_type=jnp.float32)
        here = pl.ds(j * wide, wide)
        keep_ref[:, here] = product[:half]
        send_ref[:, here] = product[half:].astype(send_ref.dtype)


def lowrank_part(left, grad_out, at, parts):
    ranks, tokens = left.shape
    columns = grad_out.shape[1] // parts
    whole = pl.BlockSpec(memory_space=pltpu.VMEM)
    return pl.pallas_call(
        functools.partial(lowrank_body, at * columns, 4),
        in_specs=[whole] * 2,
        out_specs=[whole] * 2,
        out_shape=[pltpu.VMEM((ranks // 2, columns), jnp.float32), pltpu.VMEM((ranks // 2, columns), jnp.bfloat16)],
        compiler_params=pltpu.CompilerParams(vmem_limit_bytes=KERNEL_VMEM),
        cost_estimate=pl.CostEstimate(
            flops=2 * ranks * tokens * columns, bytes_accessed=tokens * columns * 2 + ranks * columns * 3, transcendentals=0
        ),
        name="lowrank_part",
    )(in_vmem(left), in_vmem(grad_out))


def delta_body(first, tiles, basis_ref, *refs):
    *held, out_ref, buffer, sems = refs
    wide = buffer.shape[1] // tiles
    copies = []
    for j in range(tiles):
        here = pl.ds(j * wide, wide)
        ranks = jnp.concatenate([piece[:, here] for piece in held], 0)
        buffer[:, here] = jnp.dot(basis_ref[...], ranks, preferred_element_type=jnp.float32).astype(buffer.dtype)
        copy = pltpu.make_async_copy(buffer.at[:, here], out_ref.at[:, pl.ds(first + j * wide, wide)], sems.at[j])
        copy.start()
        copies.append(copy)
    for copy in copies:
        copy.wait()


def delta_next(first, tiles, basis_ref, before_ref, *refs):
    delta_body(first, tiles, basis_ref, *refs)


def delta_part(basis, held, at, parts, before):
    rows, ranks = basis.shape
    columns = held[0].shape[1]
    tiles = 4
    whole = pl.BlockSpec(memory_space=pltpu.VMEM)
    anywhere = pl.BlockSpec(memory_space=pl.ANY)
    earlier = [] if before is None else [before]
    return pl.pallas_call(
        functools.partial(delta_next if earlier else delta_body, at * columns, tiles),
        in_specs=[whole, *[anywhere] * len(earlier), *[whole] * len(held)],
        out_specs=anywhere,
        out_shape=jax.ShapeDtypeStruct((rows, parts * columns), jnp.bfloat16),
        scratch_shapes=[pltpu.VMEM((rows, columns), jnp.bfloat16), pltpu.SemaphoreType.DMA((tiles,))],
        input_output_aliases={1: 0} if earlier else {},
        compiler_params=pltpu.CompilerParams(vmem_limit_bytes=KERNEL_VMEM),
        cost_estimate=pl.CostEstimate(
            flops=2 * ranks * rows * columns, bytes_accessed=2 * (ranks + rows) * columns, transcendentals=0
        ),
        name="delta_part",
    )(in_vmem(basis), *earlier, *map(in_vmem, held))


def gathered_basis(basis):
    z, y, c = (lax.axis_index(a) for a in DP)
    odd = z % 2 == 1
    same, flipped = (lax.ppermute(basis, ALL, crossing(flip)) for flip in (0, 1))
    pair = jnp.stack([jnp.where(odd, flipped, same), jnp.where(odd, same, flipped)])
    pieces = [pair]
    for far in (2, 1, 3):
        to = [((i * C + k), (i + far) % Y * C + (k + far) % C) for i in range(Y) for k in range(C)]
        pieces.append(lax.ppermute(pair, ("y", "c"), to))
    own = jnp.stack(pieces)
    other = lax.ppermute(own, "c", [(0, 1), (1, 0)])
    whole = jnp.zeros((2, Y, C, *basis.shape), basis.dtype)
    for core, some in ((c, own), (1 - c, other)):
        for at, far in enumerate((0, 2, 1, 3)):
            place_at = (0, (y + Y - far) % Y, (core + far) % C, 0, 0)
            whole = lax.dynamic_update_slice(whole, some[at][:, None, None], place_at)
    return whole.reshape(-1, basis.shape[1])


def x_pairs(offset):
    return [(c * X + x, c * X + paired(x, X, offset + c, 1)) for c in range(C) for x in range(X)]


def exchanged(x, step):
    return lax.ppermute(x, DP, swap(step))


def joined(pieces, axis):
    return lax.optimization_barrier(jnp.concatenate(pieces, axis))


def shared_lowrank(keep, send):
    f32, bf16 = jnp.float32, jnp.bfloat16
    keep, send = list(keep), list(send)
    steps_left = len(HALVING[0])
    for at in range(steps_left):
        for k, steps in enumerate(HALVING):
            came = exchanged(send[k], steps[at])
            half = came.shape[0] // 2
            if at + 1 < steps_left:
                send[k] = (keep[k][half:] + came[half:].astype(f32)).astype(bf16)
                keep[k] = keep[k][:half] + came[:half].astype(f32)
            else:
                keep[k] = keep[k] + came.astype(f32)
    return keep


def update_body(parts, came_ref, own_ref, other_ref, *refs):
    kept, outs = refs[:parts], refs[parts:]
    first_ref, second_ref, *normalized = outs
    rows, columns = first_ref.shape
    first_fix = 1.0 - first_decay**STEP
    second_fix = 1.0 - second_decay**STEP
    wide = columns // parts
    for k in range(parts):
        here = pl.ds(k * wide, wide)
        came = came_ref[:, here]
        held = kept[k][...]
        values = []
        for at, moments in enumerate((own_ref, other_ref)):
            there = 1 - at
            lowrank = held[at * rows : (at + 1) * rows] + came[there * rows : (there + 1) * rows]
            new_first = first_decay * moments[0, :, here] + (1.0 - first_decay) * lowrank
            new_second = second_decay * moments[1, :, here] + (1.0 - second_decay) * lowrank * lowrank
            values.append(new_first / first_fix / (jnp.sqrt(new_second / second_fix) + epsilon_term))
            if at == 0:
                first_ref[:, here] = new_first
                second_ref[:, here] = new_second
        normalized[k][...] = jnp.concatenate(values, 0)


def updated(kept, came, own, other):
    shape = own.shape[1:]
    whole = pl.BlockSpec(memory_space=pltpu.VMEM)
    return pl.pallas_call(
        functools.partial(update_body, len(kept)),
        in_specs=[whole] * (3 + len(kept)),
        out_specs=[whole] * (2 + len(kept)),
        out_shape=[
            *[jax.ShapeDtypeStruct(shape, jnp.float32)] * 2,
            *(pltpu.VMEM(part.shape, jnp.float32) for part in kept),
        ],
        compiler_params=pltpu.CompilerParams(vmem_limit_bytes=KERNEL_VMEM),
        cost_estimate=pl.CostEstimate(flops=60 * own.size, bytes_accessed=20 * own.size, transcendentals=own.size),
        name="updated",
    )(in_vmem(came), in_vmem(own), in_vmem(other), *map(in_vmem, kept))


def spread(parts):
    for at in reversed(range(2, len(HALVING[0]))):
        parts = [joined([part, exchanged(part, steps[at])], 0) for part, steps in zip(parts, HALVING)]
    came = [exchanged(part, steps[1]) for part, steps in zip(parts, HALVING)]
    pieces = []
    for part, new, steps in zip(parts, came, HALVING):
        pieces += [part, new, exchanged(part, steps[0]), exchanged(new, steps[0])]
    return pieces


def on_device(features, grad_out, basis, first_moment, second_moment):
    me = place(*(lax.axis_index(a) for a in DP))
    rows = first_moment.shape[0]
    table = lax.dynamic_index_in_dim(jnp.asarray(rank_table(rows)), me, 0, keepdims=False)
    parts, ranks = table.shape
    chosen = (lax.broadcasted_iota(jnp.int32, (parts, ranks, ranks), 1) == table[:, None, :]).astype(jnp.bfloat16)
    ordered_basis = jnp.einsum("dr,krp->kdp", basis, chosen, preferred_element_type=jnp.float32).astype(jnp.bfloat16)

    met, chosen, ordered_basis = lax.optimization_barrier((gathered_basis(basis), chosen, ordered_basis))
    total = jnp.dot(features, met, preferred_element_type=jnp.float32)
    sent, grad_out, *both = lax.optimization_barrier((total.astype(jnp.bfloat16), grad_out, first_moment, second_moment))
    total = total + lax.ppermute(sent, ("c", "x"), x_pairs(0)).astype(jnp.float32)
    moments = jnp.stack(both)
    sent, grad_out = lax.optimization_barrier((total.astype(jnp.bfloat16), staged(grad_out)))
    total = total + lax.ppermute(sent, ("c", "x"), x_pairs(1)).astype(jnp.float32)
    projected = total.astype(jnp.bfloat16)
    other_moments = exchanged(moments.astype(jnp.float16), LAST)
    left = jnp.einsum("krp,tr->kpt", chosen, projected, preferred_element_type=jnp.float32).astype(jnp.bfloat16)

    keep, send = zip(*(lowrank_part(left[k], grad_out, k, parts) for k in range(parts)))

    send, other_moments = lax.optimization_barrier((send, other_moments))
    other_moments = other_moments.astype(jnp.float32)
    kept = shared_lowrank(keep, send)
    came = exchanged(jnp.concatenate([part.astype(jnp.bfloat16) for part in kept], 1), LAST)
    new_first, new_second, *normalized = updated(kept, came.astype(jnp.float32), moments, other_moments)
    pieces = spread([part.astype(jnp.bfloat16) for part in normalized])
    each = len(pieces) // parts
    delta = None
    for k in range(parts):
        delta = delta_part(ordered_basis[k], pieces[k * each : (k + 1) * each], k, parts, delta)
    return (delta, new_first, new_second)


def solution(mesh):
    fine = Mesh(mesh.devices.reshape(Z, Y, C, X), ALL)
    rows_columns = P(DP, "x")
    in_specs = (rows_columns, rows_columns, P(DP, None), rows_columns, rows_columns)
    return jax.shard_map(
        on_device, mesh=fine, in_specs=in_specs, out_specs=(rows_columns,) * 3, check_vma=False
    )
```
